32 devices in a mesh: seq: 4 (over y, core), batch: 8 (over z, x).
Axes of the slice: x: 2, y: 2, z: 4, core: 2. Of those that a mesh axis runs over, the one named last changes fastest.
Arguments:
- tower: bfloat16 [6144, 1536], P(('batch', 'seq')), parts along dimension 0, may hold values from -6 to 6
- dna: int32 [6144, 128], P(('batch', 'seq')), parts along dimension 0, may hold values from 0 to 3
- dna_weight: float32 [4, 1536], replicated, may hold values from -3 to 3
- conv_gain: float32 [1536], replicated, may hold values from 0.25 to 1.75
- depthwise_kernel: float32 [5, 1536], replicated, may hold values from -2.5 to 2.5
- attn_gain: float32 [1536], replicated, may hold values from 0.25 to 1.75
- query_weight: bfloat16 [1536, 1024], P('seq'), may hold values from -1 to 1
- key_weight: bfloat16 [1536, 128], P('seq'), may hold values from -1 to 1
- value_weight: bfloat16 [1536, 192], P('seq'), may hold values from -0.15625 to 0.15625
- out_weight: bfloat16 [1536, 1536], P('seq'), may hold values from -0.15625 to 0.15625
- pair_in_weight: bfloat16 [1536, 256], replicated, may hold values from -0.15625 to 0.15625
- pair_weight: bfloat16 [128, 128], replicated, may hold values from -0.5 to 0.5
Outputs:
- stream_out: bfloat16 [6144, 1536], P(('batch', 'seq')), parts along dimension 0
- pair: bfloat16 [384, 48, 128], P(('batch', 'seq')), parts along dimension 0
The draws below stay inside these ranges and needn't reach their ends.
There are 8 independent parts, one for each index of `batch`. The reference program is written for one: setup_inputs(seed, part) draws one part's arguments, and reference() takes and returns one part's arrays. A program takes and returns all parts, laid end to end along the dimension named above; an argument that names none is the same for every part. Nothing has to cross between parts.
All inputs are finite; a program needn't handle non-finite values.
Results may differ from the reference program's by a relative error of at most 0.013.
Values may be sent and summed in bfloat16 or wider, within the bound.
A program may use at most 64 MiB of HBM per device.

```python
import math
import jax
import jax.numpy as jnp
from jax import lax

C = 1536
H = 8
DK = 128
DV = 192
PC = 128
BASES = 128
POOL = 16
KERNEL_TAPS = 5
DILATION_STEP = 4
SEQ = 768


def draw_tower(key, part):
    return jnp.clip(jax.random.normal(jax.random.fold_in(key, 1), (SEQ, C), jnp.float32), -6.0, 6.0).astype(jnp.bfloat16)


def draw_query_weight(key, part):
    spread = C ** (-0.5)
    return (jnp.clip(jax.random.normal(jax.random.fold_in(key, 5), (C, H * DK), jnp.float32), -6.0, 6.0) * spread).astype(jnp.bfloat16)


def draw_key_weight(key, part):
    spread = C ** (-0.5)
    return (jnp.clip(jax.random.normal(jax.random.fold_in(key, 7), (C, DK), jnp.float32), -6.0, 6.0) * spread).astype(jnp.bfloat16)


def with_ends(drawn, rng, smallest, largest):
    extent = drawn.shape
    place = [jax.random.randint(jax.random.fold_in(rng, axis), (), 0, extent[axis]) for axis in range(len(extent))]
    drawn = drawn.at[tuple(place)].set(smallest)
    longest = extent.index(max(extent))
    place[longest] = (place[longest] + 1) % extent[longest]
    return drawn.at[tuple(place)].set(largest)


def block_scale(key, extent, cuts, smallest, top_value):
    loudness, own = 1.0, jax.random.fold_in(key, 6)
    for axis_at, shards_of in cuts:
        heights = jnp.exp(jax.random.uniform(jax.random.fold_in(own, axis_at), (shards_of,), jnp.float32, smallest / len(cuts), top_value / len(cuts)))
        loudness = loudness * jnp.repeat(heights, extent[axis_at] // shards_of).reshape([-1 if axis == axis_at else 1 for axis in range(len(extent))])
    return loudness


def scatter_about(own_key, dims, scale, reach, pieces=(), held_as=jnp.bfloat16):
    values = scale * jax.random.normal(own_key, dims, jnp.float32)
    if pieces:
        values = values * block_scale(own_key, dims, pieces, -0.22, 0.18)
    return jnp.clip(values, -reach, reach).astype(held_as)


def setup_inputs(seed: int = 0, part: int = 0) -> dict:
    streams_of = jax.random.split(jax.random.key(seed), 13)
    part_keys = jax.random.split(jax.random.fold_in(streams_of[12], part), 13)
    return {
        "tower": draw_tower(jax.random.fold_in(jax.random.fold_in(streams_of[12], part), 71), part),
        "dna": with_ends(jax.random.randint(part_keys[1], (SEQ, BASES), 0, 4), jax.random.fold_in(part_keys[1], 1), 0, 3).astype(jnp.int32),
        "dna_weight": scatter_about(streams_of[2], (4, C), 4 ** -0.5, 3.0, (), jnp.float32),
        "conv_gain": jnp.clip(1.0 + 0.15 * jax.random.normal(streams_of[3], (C,), jnp.float32), 0.25, 1.75),
        "depthwise_kernel": scatter_about(streams_of[4], (KERNEL_TAPS, C), KERNEL_TAPS ** -0.5, 2.5, (), jnp.float32),
        "attn_gain": jnp.clip(1.0 + 0.15 * jax.random.normal(streams_of[5], (C,), jnp.float32), 0.25, 1.75),
        "query_weight": draw_query_weight(jax.random.fold_in(streams_of[12], 71), part),
        "key_weight": draw_key_weight(jax.random.fold_in(streams_of[12], 71), part),
        "value_weight": scatter_about(streams_of[8], (C, DV), C ** -0.5, 0.15625, ((0, 4),)),
        "out_weight": scatter_about(streams_of[9], (C, C), C ** -0.5, 0.15625, ((0, 4),)),
        "pair_in_weight": scatter_about(streams_of[10], (C, 2 * PC), C ** -0.5, 0.15625),
        "pair_weight": scatter_about(streams_of[11], (PC, PC), PC ** -0.5, 0.5),
    }


def rms_norm(values, gain):
    wide = values.astype(jnp.float32)
    return wide * lax.rsqrt(lax.optimization_barrier(jnp.mean(wide * wide, axis=-1, keepdims=True)) + 1e-06) * gain

def reference(tower, dna, dna_weight, conv_gain, depthwise_kernel, attn_gain, query_weight, key_weight, value_weight, out_weight, pair_in_weight, pair_weight):
    row_length = tower.shape[0]
    counts = lax.optimization_barrier(jnp.sum((dna[:, :, None] == jnp.arange(4, dtype=jnp.int32)[None, None, :]).astype(jnp.float32), axis=1))
    composition = (counts - BASES / 4.0) * (4.0 / math.sqrt(3.0 * BASES))
    stream = tower.astype(jnp.float32) + jnp.dot(composition, dna_weight, precision=lax.Precision.HIGHEST)
    normed = rms_norm(stream, conv_gain).astype(jnp.bfloat16)
    kernel_reach = DILATION_STEP * (KERNEL_TAPS - 1) // 2
    padded_rows = jnp.pad(normed.astype(jnp.float32), ((kernel_reach, kernel_reach), (0, 0)))
    convolved_rows = jnp.zeros_like(stream)
    for kernel_tap in range(KERNEL_TAPS):
        convolved_rows = convolved_rows + depthwise_kernel[kernel_tap] * padded_rows[kernel_tap * DILATION_STEP:kernel_tap * DILATION_STEP + row_length]
    conv_out = (stream + jax.nn.gelu(convolved_rows)).astype(jnp.bfloat16)
    attn_in = rms_norm(conv_out, attn_gain).astype(jnp.bfloat16)
    queries = jnp.dot(attn_in, query_weight, preferred_element_type=jnp.float32).astype(jnp.bfloat16)
    keys = jnp.dot(attn_in, key_weight, preferred_element_type=jnp.float32).astype(jnp.bfloat16)
    values = jnp.dot(attn_in, value_weight, preferred_element_type=jnp.float32).astype(jnp.bfloat16)
    block = math.gcd(row_length, 512)
    query_blocks = queries.reshape(row_length // block, block, H, DK)
    keys_wide = keys.astype(jnp.float32)
    values_wide = values.astype(jnp.float32)

    def attend(query_block):
        scores = jnp.einsum('bhd,td->bht', query_block.astype(jnp.float32), keys_wide) / math.sqrt(DK)
        top = lax.optimization_barrier(jnp.max(scores, axis=-1, keepdims=True))
        expo = jnp.exp(scores - top)
        total = lax.optimization_barrier(jnp.sum(expo, axis=-1))
        rounded = lax.optimization_barrier(expo.astype(jnp.bfloat16)).astype(jnp.float32)
        summed = jnp.einsum('bht,te->bhe', rounded, values_wide)
        return (summed / total[:, :, None]).reshape(block, H * DV).astype(jnp.bfloat16)
    context = lax.map(attend, query_blocks).reshape(row_length, H * DV)
    stream_out = (conv_out.astype(jnp.float32) + jnp.dot(context, out_weight, preferred_element_type=jnp.float32)).astype(jnp.bfloat16)
    pooled = lax.optimization_barrier(jnp.mean(stream_out.astype(jnp.float32).reshape(row_length // POOL, POOL, -1), axis=1)).astype(jnp.bfloat16)
    features = jnp.dot(pooled, pair_in_weight, preferred_element_type=jnp.float32).astype(jnp.bfloat16)
    width = pair_weight.shape[0]
    left = features[:, :width].astype(jnp.float32)
    right = features[:, width:].astype(jnp.float32)
    outer = (left[:, None, :] * right[None, :, :]).astype(jnp.bfloat16)
    mixed = jnp.einsum('ijc,cd->ijd', outer.astype(jnp.float32), pair_weight.astype(jnp.float32))
    pair = (mixed + left[:, None, :] + right[None, :, :]).astype(jnp.bfloat16)
    return (stream_out, pair)
```

```python
import functools
import math

import jax
import jax.numpy as jnp
from jax import lax
from jax.experimental import pallas as pl
from jax.experimental.pallas import tpu as pltpu
from jax.sharding import PartitionSpec as P

H = 8
DK = 128
DV = 192
BASES = 128
POOL = 16
KERNEL_TAPS = 5
DILATION_STEP = 4
REACH = DILATION_STEP * (KERNEL_TAPS - 1) // 2
EDGE = 16
PAIRS = H // 2
F32 = jnp.float32
BF16 = jnp.bfloat16


def cut(rows, most):
    parts = most
    while rows % parts or (rows // parts) % 16:
        parts -= 1
    return parts


def kernel(
    n,
    tower,
    dna,
    dna_weight,
    conv_gain,
    taps,
    attn_gain,
    query_hbm,
    key_hbm,
    value_hbm,
    out_hbm,
    pair_in_hbm,
    pair_hbm,
    out_ref,
    pair_ref,
    wk,
    wv,
    wq,
    wo,
    pair_in,
    pair_w,
    stream_s,
    padded,
    edges,
    halo,
    conv_s,
    attn_s,
    q_s,
    k_all,
    v_all,
    ctx_s,
    pooled_s,
    left_s,
    slots,
    right_s,
    outer_s,
    halo_sem,
    local_sem,
    own_sem,
    y_send,
    y_recv,
    x_send,
    x_recv,
    f_send,
    f_recv,
    g_send,
    g_recv,
    kv_send,
    kv_recv,
    r_send,
    r_recv,
):
    rows, channels = tower.shape
    seq = lax.axis_index("seq")
    batch = lax.axis_index("batch")
    chips = n // 2
    y, core = seq // 2, lax.rem(seq, 2)
    parity = lax.rem(batch, 2)
    x_other = batch + 1 - 2 * parity
    c_other = seq + 1 - 2 * core

    def at(s, b):
        return {"seq": s, "batch": b}

    hbm = (key_hbm, value_hbm, query_hbm, out_hbm)
    full = (wk, wv, wq, wo)
    block = query_hbm.shape[0]
    half = block // 2
    q_parts, o_parts = cut(half, 2), cut(half, PAIRS)
    q_len, o_len = half // q_parts, half // o_parts
    q_first, o_first = 2, 2 + q_parts

    def span(owner, side, offset, length):
        return pl.ds(pl.multiple_of(owner * block + side * half + offset, 16), length)

    def piece(index):
        if not isinstance(index, int):
            return 3, (index - o_first) * o_len, o_len
        if index < 2:
            return index, 0, half
        if index < o_first:
            return 2, (index - q_first) * q_len, q_len
        return 3, (index - o_first) * o_len, o_len

    def remote(src, dst, send, recv, where):
        return pltpu.make_async_remote_copy(
            src_ref=src,
            dst_ref=dst,
            send_sem=send,
            recv_sem=recv,
            device_id=where,
            device_id_type=pl.DeviceIdType.MESH,
        )

    def held(index, owner, side):
        which, offset, length = piece(index)
        return full[which].at[span(owner, side, offset, length), :]

    def y_copy(j, index):
        which, offset, length = piece(index)
        src = hbm[which].at[pl.ds(pl.multiple_of(parity * half + offset, 16), length), :]
        to = lax.rem(y + j, chips) * 2 + core
        return remote(src, held(index, seq, parity), y_send.at[j - 1, index], y_recv.at[j - 1, index], at(to, batch))

    def source(j):
        return lax.rem(y + chips - j, chips) * 2

    def y_arrived(j, index):
        ref = held(index, source(j) + core, parity)
        return remote(ref, ref, y_send.at[j - 1, index], y_recv.at[j - 1, index], at(seq, batch))

    def x_copy(j, index, side):
        ref = held(index, source(j) + core, side)
        return remote(ref, ref, x_send.at[j - 1, index], x_recv.at[j - 1, index], at(seq, x_other))

    def f_copy(j, index, who):
        ref = held(index, source(j) + who, parity)
        return remote(ref, ref, f_send.at[j - 1, index], f_recv.at[j - 1, index], at(c_other, batch))

    def g_copy(j, index, who):
        ref = held(index, source(j) + who, 1 - parity)
        return remote(ref, ref, g_send.at[j - 1, index], g_recv.at[j - 1, index], at(c_other, batch))

    def own_copy(which, owner):
        ref = full[which].at[pl.ds(pl.multiple_of(owner * block, 16), block), :]
        return remote(hbm[which], ref, own_sem.at[0, which], own_sem.at[1, which], at(c_other, batch))

    def local_copy(which):
        ref = full[which].at[pl.ds(pl.multiple_of(seq * block, 16), block), :]
        return pltpu.make_async_copy(hbm[which], ref, local_sem.at[which])

    def from_y(index):
        for j in range(1, chips):
            y_arrived(j, index).wait_recv()
            x_copy(j, index, parity).start()
            f_copy(j, index, core).start()

    def from_x(index):
        for j in range(1, chips):
            x_copy(j, index, 1 - parity).wait_recv()
            g_copy(j, index, core).start()

    def from_core(index):
        for j in range(1, chips):
            f_copy(j, index, 1 - core).wait_recv()
            g_copy(j, index, 1 - core).wait_recv()

    barrier = pltpu.get_barrier_semaphore()
    for k in range(1, n):
        pl.semaphore_signal(
            barrier, inc=1, device_id=at(lax.rem(seq + k, n), batch), device_id_type=pl.DeviceIdType.MESH
        )
    pl.semaphore_signal(barrier, inc=1, device_id=at(seq, x_other), device_id_type=pl.DeviceIdType.MESH)
    for which in range(4):
        local_copy(which).start()
    pair_in_copy = pltpu.make_async_copy(pair_in_hbm, pair_in, local_sem.at[4])
    pair_copy = pltpu.make_async_copy(pair_hbm, pair_w, local_sem.at[5])
    pair_in_copy.start()
    pair_copy.start()

    def normalise(first, count, width):
        rows_at = pl.ds(first, count)
        bases = dna[rows_at, :]
        shares = [
            (jnp.sum((bases == b).astype(F32), axis=1, keepdims=True) - BASES / 4.0)
            * (4.0 / math.sqrt(3.0 * BASES))
            for b in range(4)
        ]

        def add(i, total):
            cols = pl.ds(pl.multiple_of(i * width, 128), width)
            value = tower[rows_at, cols].astype(F32)
            for b in range(4):
                value = value + shares[b] * dna_weight[pl.ds(b, 1), cols]
            stream_s[rows_at, cols] = value
            square = value * value
            for g in range(width // 128):
                total = total + square[:, g * 128 : (g + 1) * 128]
            return total

        total = lax.fori_loop(0, channels // width, add, jnp.zeros((count, 128), F32))
        factor = lax.rsqrt(jnp.sum(total, axis=1, keepdims=True) * (1.0 / channels) + 1e-6)

        def scale(i, carry):
            cols = pl.ds(pl.multiple_of(i * width, 128), width)
            value = (stream_s[rows_at, cols] * factor * conv_gain[:, cols]).astype(BF16)
            padded[pl.ds(REACH + first, count), cols] = value.astype(F32)
            if first == 0:
                edges[0, :, cols] = value
            elif first == rows - EDGE:
                edges[1, :, cols] = value
            return carry

        lax.fori_loop(0, channels // width, scale, 0)

    normalise(0, EDGE, channels)
    normalise(rows - EDGE, EDGE, channels)

    pl.semaphore_wait(barrier, n)

    to_left = remote(edges.at[0], halo.at[1], halo_sem.at[0], halo_sem.at[1], at(jnp.maximum(seq - 1, 0), batch))
    to_right = remote(edges.at[1], halo.at[0], halo_sem.at[2], halo_sem.at[3], at(jnp.minimum(seq + 1, n - 1), batch))

    @pl.when(seq > 0)
    def _():
        to_left.start()

    @pl.when(seq < n - 1)
    def _():
        to_right.start()

    for index in range(o_first):
        for j in range(1, chips):
            y_copy(j, index).start()
    for which in range(3):
        own_copy(which, seq).start()
    for index in range(o_first, o_first + o_parts):
        for j in range(1, chips):
            y_copy(j, index).start()

    normalise(EDGE, rows - 2 * EDGE, 128)
    from_y(0)
    from_y(1)

    @pl.when(seq > 0)
    def _():
        to_right.wait_recv()
        padded[pl.ds(0, REACH), :] = halo[0].astype(F32)[EDGE - REACH :]

    @pl.when(seq == 0)
    def _():
        padded[pl.ds(0, REACH), :] = jnp.zeros((REACH, channels), F32)

    @pl.when(seq < n - 1)
    def _():
        to_left.wait_recv()
        padded[pl.ds(REACH + rows, REACH), :] = halo[1].astype(F32)[:REACH]

    @pl.when(seq == n - 1)
    def _():
        padded[pl.ds(REACH + rows, REACH), :] = jnp.zeros((REACH, channels), F32)

    def convolve(i, total):
        cols = pl.ds(pl.multiple_of(i * 128, 128), 128)
        value = jnp.zeros((rows, 128), F32)
        for t in range(KERNEL_TAPS):
            value = value + taps[pl.ds(t, 1), cols] * padded[pl.ds(t * DILATION_STEP, rows), cols]
        inner = math.sqrt(2.0 / math.pi) * (value + 0.044715 * (value * value * value))
        value = (stream_s[:, cols] + value * (0.5 + 0.5 * jnp.tanh(inner))).astype(BF16)
        conv_s[:, cols] = value
        value = value.astype(F32)
        return total + value * value

    total = lax.fori_loop(0, channels // 128, convolve, jnp.zeros((rows, 128), F32))
    factor = lax.rsqrt(jnp.sum(total, axis=1, keepdims=True) * (1.0 / channels) + 1e-6)

    def renormalise(i, carry):
        cols = pl.ds(pl.multiple_of(i * 128, 128), 128)
        attn_s[:, cols] = (conv_s[:, cols].astype(F32) * factor * attn_gain[:, cols]).astype(BF16)
        return carry

    lax.fori_loop(0, channels // 128, renormalise, 0)

    from_x(0)
    from_x(1)
    from_y(2)
    for which in range(2):
        local_copy(which).wait()
        own_copy(which, c_other).wait_recv()
        from_core(which)
    mine = pl.ds(pl.multiple_of(seq * rows, 16), rows)
    attn_in = attn_s[...]
    k_all[mine, :] = jnp.dot(attn_in, wk[...], preferred_element_type=F32).astype(BF16)
    v_all[mine, :] = jnp.dot(attn_in, wv[...], preferred_element_type=F32).astype(BF16)

    def kv_copy(k, which, owner):
        ref = (k_all, v_all)[which].at[pl.ds(pl.multiple_of(owner * rows, 16), rows), :]
        return remote(ref, ref, kv_send.at[k - 1, which], kv_recv.at[k - 1, which], at(lax.rem(seq + k, n), batch))

    for k in range(1, n):
        for which in range(2):
            kv_copy(k, which, seq).start()
    own_copy(3, seq).start()

    for index in range(3, o_first):
        from_y(index)
    for index in range(2, o_first):
        from_x(index)
    local_copy(2).wait()
    own_copy(2, c_other).wait_recv()
    for index in range(2, o_first):
        from_core(index)

    def query(p, carry):
        cols = pl.ds(pl.multiple_of(p * 2 * DK, 2 * DK), 2 * DK)
        value = jnp.dot(attn_s[...], wq[:, cols], preferred_element_type=F32).astype(BF16)
        q_s[p, pl.ds(0, rows), :] = value[:, :DK]
        q_s[p, pl.ds(rows, rows), :] = value[:, DK:]
        return carry

    lax.fori_loop(0, PAIRS, query, 0)
    for k in range(1, n):
        owner = lax.rem(seq + n - k, n)
        for which in range(2):
            kv_copy(k, which, owner).wait_recv()

    to_power = math.log2(math.e) / math.sqrt(DK)

    def attend(p, carry):
        scores = lax.dot_general(
            q_s[p], k_all[...], (((1,), (1,)), ((), ())), preferred_element_type=F32
        )
        top = jnp.max(scores, axis=1, keepdims=True)
        expo = jnp.exp2((scores - top) * to_power)
        sums = jnp.sum(expo, axis=1, keepdims=True)
        value = jnp.dot(expo.astype(BF16), v_all[...], preferred_element_type=F32)
        value = (value / sums).astype(BF16)
        ctx_s[p, :, pl.ds(0, DV)] = value[:rows]
        ctx_s[p, :, pl.ds(DV, DV)] = value[rows:]
        if o_parts == PAIRS:
            from_y(o_first + p)
        return carry

    lax.fori_loop(0, PAIRS, attend, 0)
    for index in range(o_first, o_first + o_parts):
        if o_parts != PAIRS:
            from_y(index)
        from_x(index)
    local_copy(3).wait()
    own_copy(3, c_other).wait_recv()
    for index in range(o_first, o_first + o_parts):
        from_core(index)

    own_rows = rows // POOL
    pooled_s[...] = jnp.zeros_like(pooled_s)
    width = 512

    def project(i, carry):
        cols = pl.ds(pl.multiple_of(i * width, width), width)
        value = conv_s[:, cols].astype(F32)
        total = jnp.zeros((rows, width), F32)
        for p in range(PAIRS):
            total = total + jnp.dot(
                ctx_s[p], wo[pl.ds(p * 2 * DV, 2 * DV), cols], preferred_element_type=F32
            )
        value = (value + total).astype(BF16)
        out_ref[:, cols] = value
        value = value.astype(F32).reshape(own_rows, POOL, width)
        pooled_s[pl.ds(0, own_rows), cols] = jnp.sum(value, axis=1) * (1.0 / POOL)
        return carry

    lax.fori_loop(0, channels // width, project, 0)
    pair_in_copy.wait()
    pair_copy.wait()
    features = jnp.dot(pooled_s[...].astype(BF16), pair_in[...], preferred_element_type=F32).astype(BF16)
    pair_width = pair_w.shape[0]
    left_s[...] = features[:, :pair_width].astype(F32)
    slots[seq] = features[:, pair_width:]

    def r_copy(k, owner):
        ref = slots.at[owner]
        return remote(ref, ref, r_send.at[k - 1], r_recv.at[k - 1], at(lax.rem(seq + k, n), batch))

    for k in range(1, n):
        r_copy(k, seq).start()
    for index in range(o_first + o_parts):
        for j in range(1, chips):
            y_copy(j, index).wait_send()
            x_copy(j, index, parity).wait_send()
            f_copy(j, index, core).wait_send()
            g_copy(j, index, core).wait_send()
    for which in range(4):
        own_copy(which, seq).wait_send()
    for k in range(1, n):
        for which in range(2):
            kv_copy(k, which, seq).wait_send()

    @pl.when(seq > 0)
    def _():
        to_left.wait_send()

    @pl.when(seq < n - 1)
    def _():
        to_right.wait_send()

    for k in range(1, n):
        r_copy(k, lax.rem(seq + n - k, n)).wait_recv()
    for owner in range(n):
        right_s[pl.ds(owner * own_rows, own_rows), :] = slots[owner].astype(F32)[:own_rows]
    all_rows = n * own_rows
    for i in range(own_rows):
        outer_s[pl.ds(i * all_rows, all_rows), :] = (left_s[pl.ds(i, 1), :] * right_s[...]).astype(BF16)
    mixed = jnp.dot(outer_s[...], pair_w[...], preferred_element_type=F32)
    for i in range(own_rows):
        pair_ref[i] = (
            mixed[i * all_rows : (i + 1) * all_rows] + left_s[pl.ds(i, 1), :] + right_s[...]
        ).astype(BF16)
    for k in range(1, n):
        r_copy(k, seq).wait_send()


def local(
    n,
    tower,
    dna,
    dna_weight,
    conv_gain,
    depthwise_kernel,
    attn_gain,
    query_weight,
    key_weight,
    value_weight,
    out_weight,
    pair_in_weight,
    pair_weight,
):
    rows, channels = tower.shape
    block = query_weight.shape[0]
    depth = n * block
    chips = n // 2
    pair_width = pair_weight.shape[0]
    own_rows = rows // POOL
    all_rows = n * own_rows
    pieces = 2 + cut(block // 2, 2) + cut(block // 2, PAIRS)
    dma = pltpu.SemaphoreType.DMA
    vmem = pl.BlockSpec(memory_space=pltpu.VMEM)
    anywhere = pl.BlockSpec(memory_space=pl.ANY)
    return pl.pallas_call(
        functools.partial(kernel, n),
        out_shape=(
            jax.ShapeDtypeStruct((rows, channels), BF16),
            jax.ShapeDtypeStruct((own_rows, all_rows, pair_width), BF16),
        ),
        in_specs=[vmem] * 6 + [anywhere] * 6,
        out_specs=(vmem, vmem),
        scratch_shapes=[
            pltpu.VMEM((depth, DK), BF16),
            pltpu.VMEM((depth, DV), BF16),
            pltpu.VMEM((depth, H * DK), BF16),
            pltpu.VMEM((depth, out_weight.shape[1]), BF16),
            pltpu.VMEM(pair_in_weight.shape, BF16),
            pltpu.VMEM(pair_weight.shape, BF16),
            pltpu.VMEM((rows, channels), F32),
            pltpu.VMEM((rows + 2 * REACH, channels), F32),
            pltpu.VMEM((2, EDGE, channels), BF16),
            pltpu.VMEM((2, EDGE, channels), BF16),
            pltpu.VMEM((rows, channels), BF16),
            pltpu.VMEM((rows, channels), BF16),
            pltpu.VMEM((PAIRS, 2 * rows, DK), BF16),
            pltpu.VMEM((n * rows, DK), BF16),
            pltpu.VMEM((n * rows, DV), BF16),
            pltpu.VMEM((PAIRS, rows, 2 * DV), BF16),
            pltpu.VMEM((16, channels), F32),
            pltpu.VMEM((16, pair_width), F32),
            pltpu.VMEM((n, 16, pair_width), BF16),
            pltpu.VMEM((all_rows, pair_width), F32),
            pltpu.VMEM((own_rows * all_rows, pair_width), BF16),
            dma((4,)),
            dma((6,)),
            dma((2, 4)),
        ]
        + [dma((chips - 1, pieces))] * 8
        + [dma((n - 1, 2))] * 2
        + [dma((n - 1,))] * 2,
        compiler_params=pltpu.CompilerParams(
            collective_id=0, has_side_effects=True, vmem_limit_bytes=56 * 1024 * 1024
        ),
    )(
        tower,
        dna,
        dna_weight,
        conv_gain.reshape(1, channels),
        depthwise_kernel,
        attn_gain.reshape(1, channels),
        query_weight,
        key_weight,
        value_weight,
        out_weight,
        pair_in_weight,
        pair_weight,
    )


def solution(mesh):
    rows = P(("batch", "seq"), None)
    in_specs = (rows, rows, P(), P(), P(), P()) + (P("seq", None),) * 4 + (P(), P())
    out_specs = (rows, P(("batch", "seq"), None, None))
    return jax.shard_map(
        functools.partial(local, mesh.shape["seq"]),
        mesh=mesh,
        in_specs=in_specs,
        out_specs=out_specs,
        check_vma=False,
    )
```

```python
import functools
import math

import jax
import jax.numpy as jnp
from jax import lax
from jax.experimental import pallas as pl
from jax.experimental.pallas import tpu as pltpu
from jax.sharding import PartitionSpec as P

H = 8
DK = 128
DV = 192
BASES = 128
POOL = 16
KERNEL_TAPS = 5
DILATION_STEP = 4
REACH = DILATION_STEP * (KERNEL_TAPS - 1) // 2
EDGE = 16
PAIRS = H // 2
F32 = jnp.float32
BF16 = jnp.bfloat16


Y, X, Z, D = range(4)


def group_of(block):
    return 4 if block % 64 == 0 else 2


def pieces_of(block):
    groups = group_of(block)
    part = block // groups
    cuts = 2 if part % 32 == 0 else 1
    length = part // cuts
    pieces = [(0, 0, part), (1, 0, DV // groups)]
    for which in (2, 3):
        pieces += [(which, i * length, length) for i in range(cuts)]
    return pieces, 2, 2 + cuts


def kernel(
    n,
    tower,
    dna,
    dna_weight,
    conv_gain,
    taps,
    attn_gain,
    query_hbm,
    key_hbm,
    value_hbm,
    out_hbm,
    pair_in_hbm,
    pair_hbm,
    out_ref,
    pair_ref,
    wk,
    wv,
    wq,
    wo,
    pair_in,
    pair_w,
    stream_s,
    padded,
    edges,
    halo,
    conv_s,
    attn_s,
    q_s,
    k_all,
    v_all,
    ctx_s,
    pooled_s,
    left_s,
    slots,
    right_s,
    outer_s,
    gains,
    halo_sem,
    local_sem,
    own_sem,
    w_send,
    w_recv,
    kv_send,
    kv_recv,
    r_send,
    r_recv,
):
    rows, channels = tower.shape
    seq = lax.axis_index("seq")
    batch = lax.axis_index("batch")
    chips = n // 2
    y, core = seq // 2, lax.rem(seq, 2)
    by_x = lax.rem(batch, 2)
    by_z = lax.rem(batch // 2, 2)
    c_other = seq + 1 - 2 * core

    def at(s, b):
        return {"seq": s, "batch": b}

    core_peer = at(c_other, batch)
    x_peer = at(seq, batch + 1 - 2 * by_x)
    z_peer = at(seq, batch + 2 - 4 * by_z)
    hbm = (key_hbm, value_hbm, query_hbm, out_hbm)
    full = (wk, wv, wq, wo)
    block = query_hbm.shape[0]
    groups = group_of(block)
    part = block // groups
    pieces, first_query, first_out = pieces_of(block)
    mine = by_x if groups == 2 else 2 * by_z + by_x
    quarter = {Y: mine, X: mine + 1 - 2 * by_x, Z: mine + 2 - 4 * by_z, D: groups - 1 - mine}

    def remote(src, dst, send, recv, where):
        return pltpu.make_async_remote_copy(
            src_ref=src,
            dst_ref=dst,
            send_sem=send,
            recv_sem=recv,
            device_id=where,
            device_id_type=pl.DeviceIdType.MESH,
        )

    def held(index, owner, side):
        which, offset, length = pieces[index]
        if which == 1:
            return wv.at[owner, pl.ds(pl.multiple_of(side * length, 16), length), :]
        return full[which].at[pl.ds(pl.multiple_of(owner * block + side * part + offset, 16), length), :]

    def weight_copy(route, j, index, ref, where, src=None):
        sems = (w_send.at[route, j - 1, index], w_recv.at[route, j - 1, index])
        return remote(ref if src is None else src, ref, *sems, where)

    def source(j):
        return lax.rem(y + chips - j, chips) * 2

    def y_copy(j, index):
        which, offset, length = pieces[index]
        start = mine * (length if which == 1 else part) + offset
        src = hbm[which].at[pl.ds(pl.multiple_of(start, 16), length), :]
        to = lax.rem(y + j, chips) * 2 + core
        return weight_copy(Y, j, index, held(index, seq, mine), at(to, batch), src)

    def arrival(route, j, index):
        ref = held(index, source(j) + core, quarter[route])
        return weight_copy(route, j, index, ref, core_peer)

    def x_copy(j, index):
        return weight_copy(X, j, index, held(index, source(j) + core, mine), x_peer)

    def z_copy(j, index):
        return weight_copy(Z, j, index, held(index, source(j) + core, mine), z_peer)

    def d_copy(j, index):
        via, peer = (X, z_peer) if index % 2 == 0 else (Z, x_peer)
        return weight_copy(D, j, index, held(index, source(j) + core, quarter[via]), peer)

    def c_copy(route, j, index, who):
        ref = held(index, source(j) + who, quarter[route])
        return weight_copy(route + 4, j, index, ref, core_peer)

    def own_copy(which, owner):
        if which == 1:
            ref = wv.at[owner]
        else:
            ref = full[which].at[pl.ds(pl.multiple_of(owner * block, 16), block), :]
        return remote(hbm[which], ref, own_sem.at[0, which], own_sem.at[1, which], core_peer)

    def local_copy(which):
        if which == 1:
            ref = wv.at[seq]
        else:
            ref = full[which].at[pl.ds(pl.multiple_of(seq * block, 16), block), :]
        return pltpu.make_async_copy(hbm[which], ref, local_sem.at[which])

    routes = (Y, X) if groups == 2 else (Y, X, Z, D)

    def forward(route, index):
        if route not in routes:
            return
        for j in range(1, chips):
            arrival(route, j, index).wait_recv()
            if route == Y:
                x_copy(j, index).start()
                if groups == 4:
                    z_copy(j, index).start()
            if groups == 4 and route == (X if index % 2 == 0 else Z):
                d_copy(j, index).start()
            c_copy(route, j, index, core).start()

    def from_core(index):
        for j in range(1, chips):
            for route in routes:
                c_copy(route, j, index, 1 - core).wait_recv()

    q_pieces = range(first_query, first_out)
    o_pieces = range(first_out, len(pieces))

    barrier = pltpu.get_barrier_semaphore()
    for k in range(1, n):
        pl.semaphore_signal(
            barrier, inc=1, device_id=at(lax.rem(seq + k, n), batch), device_id_type=pl.DeviceIdType.MESH
        )
    pl.semaphore_signal(barrier, inc=1, device_id=x_peer, device_id_type=pl.DeviceIdType.MESH)
    if groups == 4:
        pl.semaphore_signal(barrier, inc=1, device_id=z_peer, device_id_type=pl.DeviceIdType.MESH)
    gains[pl.ds(0, 1), :] = conv_gain[...].reshape(1, channels)
    gains[pl.ds(1, 1), :] = attn_gain[...].reshape(1, channels)
    for which in range(4):
        local_copy(which).start()
    pair_in_copy = pltpu.make_async_copy(pair_in_hbm, pair_in, local_sem.at[4])
    pair_copy = pltpu.make_async_copy(pair_hbm, pair_w, local_sem.at[5])
    pair_in_copy.start()
    pair_copy.start()

    def normalise(first, count, width):
        rows_at = pl.ds(first, count)
        bases = dna[rows_at, :]
        shares = [
            (jnp.sum((bases == b).astype(F32), axis=1, keepdims=True) - BASES / 4.0)
            * (4.0 / math.sqrt(3.0 * BASES))
            for b in range(4)
        ]

        def add(i, total):
            cols = pl.ds(pl.multiple_of(i * width, 128), width)
            value = tower[rows_at, cols].astype(F32)
            for b in range(4):
                value = value + shares[b] * dna_weight[pl.ds(b, 1), cols]
            stream_s[rows_at, cols] = value
            square = value * value
            for g in range(width // 128):
                total = total + square[:, g * 128 : (g + 1) * 128]
            return total

        total = lax.fori_loop(0, channels // width, add, jnp.zeros((count, 128), F32))
        factor = lax.rsqrt(jnp.sum(total, axis=1, keepdims=True) * (1.0 / channels) + 1e-6)

        def scale(i, carry):
            cols = pl.ds(pl.multiple_of(i * width, 128), width)
            value = (stream_s[rows_at, cols] * factor * gains[pl.ds(0, 1), cols]).astype(BF16)
            padded[pl.ds(REACH + first, count), cols] = value.astype(F32)
            if first == 0:
                edges[0, :, cols] = value
            elif first == rows - EDGE:
                edges[1, :, cols] = value
            return carry

        lax.fori_loop(0, channels // width, scale, 0)

    normalise(0, EDGE, channels)
    normalise(rows - EDGE, EDGE, channels)

    pl.semaphore_wait(barrier, n if groups == 2 else n + 1)

    to_left = remote(edges.at[0], halo.at[1], halo_sem.at[0], halo_sem.at[1], at(jnp.maximum(seq - 1, 0), batch))
    to_right = remote(edges.at[1], halo.at[0], halo_sem.at[2], halo_sem.at[3], at(jnp.minimum(seq + 1, n - 1), batch))

    @pl.when(seq > 0)
    def _():
        to_left.start()

    @pl.when(seq < n - 1)
    def _():
        to_right.start()

    for index in range(first_out):
        for j in range(1, chips):
            y_copy(j, index).start()
    for which in range(3):
        own_copy(which, seq).start()
    for index in o_pieces:
        for j in range(1, chips):
            y_copy(j, index).start()

    normalise(EDGE, rows - 2 * EDGE, 128)
    for index in range(2):
        forward(Y, index)

    @pl.when(seq > 0)
    def _():
        to_right.wait_recv()
        padded[pl.ds(0, REACH), :] = halo[0].astype(F32)[EDGE - REACH :]

    @pl.when(seq == 0)
    def _():
        padded[pl.ds(0, REACH), :] = jnp.zeros((REACH, channels), F32)

    @pl.when(seq < n - 1)
    def _():
        to_left.wait_recv()
        padded[pl.ds(REACH + rows, REACH), :] = halo[1].astype(F32)[:REACH]

    @pl.when(seq == n - 1)
    def _():
        padded[pl.ds(REACH + rows, REACH), :] = jnp.zeros((REACH, channels), F32)

    def convolve(i, total):
        cols = pl.ds(pl.multiple_of(i * 128, 128), 128)
        value = jnp.zeros((rows, 128), F32)
        for t in range(KERNEL_TAPS):
            value = value + taps[pl.ds(t, 1), cols] * padded[pl.ds(t * DILATION_STEP, rows), cols]
        inner = math.sqrt(2.0 / math.pi) * (value + 0.044715 * (value * value * value))
        value = (stream_s[:, cols] + value * (0.5 + 0.5 * jnp.tanh(inner))).astype(BF16)
        conv_s[:, cols] = value
        value = value.astype(F32)
        return total + value * value

    total = lax.fori_loop(0, channels // 128, convolve, jnp.zeros((rows, 128), F32))
    factor = lax.rsqrt(jnp.sum(total, axis=1, keepdims=True) * (1.0 / channels) + 1e-6)

    for index in range(2):
        forward(X, index)
        forward(Z, index)

    def renormalise(i, carry):
        cols = pl.ds(pl.multiple_of(i * 128, 128), 128)
        attn_s[:, cols] = (conv_s[:, cols].astype(F32) * factor * gains[pl.ds(1, 1), cols]).astype(BF16)
        return carry

    lax.fori_loop(0, channels // 128, renormalise, 0)

    for index in q_pieces:
        forward(Y, index)
    for index in range(2):
        forward(D, index)
    for which in range(2):
        local_copy(which).wait()
        own_copy(which, c_other).wait_recv()
        from_core(which)
    attn_in = attn_s[...]

    def own(owner):
        return pl.ds(pl.multiple_of(owner * rows, 16), rows)

    k_all[own(seq), :] = jnp.dot(attn_in, wk[...], preferred_element_type=F32).astype(BF16)
    value = jnp.zeros((rows, DV), F32)
    for owner in range(n):
        value = value + lax.dot_general(
            attn_s[:, pl.ds(owner * block, block)],
            wv[owner],
            (((1,), (1,)), ((), ())),
            preferred_element_type=F32,
        )
    v_all[own(seq), :] = value.astype(BF16)

    def kv_copy(slot, which, owner, where):
        ref = (k_all, v_all)[which].at[own(owner), :]
        return remote(ref, ref, kv_send.at[slot, which], kv_recv.at[slot, which], where)

    def kv_sends(slot, which):
        if slot == 0:
            return kv_copy(0, which, seq, core_peer)
        if slot < chips:
            return kv_copy(slot, which, seq, at(lax.rem(y + slot, chips) * 2 + core, batch))
        return kv_copy(slot, which, source(slot - chips + 1) + core, core_peer)

    for slot in list(range(1, chips)) + [0]:
        for which in range(2):
            kv_sends(slot, which).start()
    for index in q_pieces:
        forward(X, index)
        forward(Z, index)
    own_copy(3, seq).start()
    for index in o_pieces:
        forward(Y, index)
    for index in q_pieces:
        forward(D, index)
    for j in range(1, chips):
        for which in range(2):
            kv_copy(j, which, source(j) + core, core_peer).wait_recv()
            kv_sends(chips - 1 + j, which).start()
    local_copy(2).wait()
    own_copy(2, c_other).wait_recv()
    for index in q_pieces:
        from_core(index)

    def query(p, carry):
        cols = pl.ds(pl.multiple_of(p * 2 * DK, 2 * DK), 2 * DK)
        value = jnp.dot(attn_s[...], wq[:, cols], preferred_element_type=F32).astype(BF16)
        q_s[p, pl.ds(0, rows), :] = value[:, :DK]
        q_s[p, pl.ds(rows, rows), :] = value[:, DK:]
        return carry

    lax.fori_loop(0, PAIRS, query, 0)
    for which in range(2):
        kv_copy(0, which, c_other, core_peer).wait_recv()
        for j in range(1, chips):
            kv_copy(chips - 1 + j, which, source(j) + 1 - core, core_peer).wait_recv()

    to_power = math.log2(math.e) / math.sqrt(DK)

    def attend(p, carry):
        scores = lax.dot_general(
            q_s[p], k_all[...], (((1,), (1,)), ((), ())), preferred_element_type=F32
        )
        top = jnp.max(scores, axis=1, keepdims=True)
        expo = jnp.exp2((scores - top) * to_power)
        sums = jnp.sum(expo, axis=1, keepdims=True)
        value = jnp.dot(expo.astype(BF16), v_all[...], preferred_element_type=F32)
        value = (value / sums).astype(BF16)
        ctx_s[p, :, pl.ds(0, DV)] = value[:rows]
        ctx_s[p, :, pl.ds(DV, DV)] = value[rows:]

        for index in o_pieces:

            @pl.when(p == index - first_out)
            def _():
                forward(X, index)
                forward(Z, index)

            @pl.when(p == index - first_out + 2)
            def _():
                forward(D, index)

        return carry

    lax.fori_loop(0, PAIRS, attend, 0)
    local_copy(3).wait()
    own_copy(3, c_other).wait_recv()
    for index in o_pieces:
        from_core(index)

    own_rows = rows // POOL
    pooled_s[...] = jnp.zeros_like(pooled_s)
    width = 512

    def project(i, carry):
        cols = pl.ds(pl.multiple_of(i * width, width), width)
        value = conv_s[:, cols].astype(F32)
        total = jnp.zeros((rows, width), F32)
        for p in range(PAIRS):
            total = total + jnp.dot(
                ctx_s[p], wo[pl.ds(p * 2 * DV, 2 * DV), cols], preferred_element_type=F32
            )
        value = (value + total).astype(BF16)
        out_ref[:, cols] = value
        value = value.astype(F32).reshape(own_rows, POOL, width)
        pooled_s[pl.ds(0, own_rows), cols] = jnp.sum(value, axis=1) * (1.0 / POOL)
        return carry

    lax.fori_loop(0, channels // width, project, 0)
    pair_in_copy.wait()
    pair_copy.wait()
    features = jnp.dot(pooled_s[...].astype(BF16), pair_in[...], preferred_element_type=F32).astype(BF16)
    pair_width = pair_w.shape[0]
    left_s[...] = features[:, :pair_width].astype(F32)
    slots[seq] = features[:, pair_width:]

    def r_copy(k, owner):
        ref = slots.at[owner]
        return remote(ref, ref, r_send.at[k - 1], r_recv.at[k - 1], at(lax.rem(seq + k, n), batch))

    for k in range(1, n):
        r_copy(k, seq).start()
    for index in range(len(pieces)):
        for j in range(1, chips):
            y_copy(j, index).wait_send()
            x_copy(j, index).wait_send()
            if groups == 4:
                z_copy(j, index).wait_send()
                d_copy(j, index).wait_send()
            for route in routes:
                c_copy(route, j, index, core).wait_send()
    for which in range(4):
        own_copy(which, seq).wait_send()
    for slot in range(2 * chips - 1):
        for which in range(2):
            kv_sends(slot, which).wait_send()

    @pl.when(seq > 0)
    def _():
        to_left.wait_send()

    @pl.when(seq < n - 1)
    def _():
        to_right.wait_send()

    for k in range(1, n):
        r_copy(k, lax.rem(seq + n - k, n)).wait_recv()
    for owner in range(n):
        right_s[pl.ds(owner * own_rows, own_rows), :] = slots[owner].astype(F32)[:own_rows]
    all_rows = n * own_rows
    for i in range(own_rows):
        outer_s[pl.ds(i * all_rows, all_rows), :] = (left_s[pl.ds(i, 1), :] * right_s[...]).astype(BF16)
    mixed = jnp.dot(outer_s[...], pair_w[...], preferred_element_type=F32)
    for i in range(own_rows):
        pair_ref[i] = (
            mixed[i * all_rows : (i + 1) * all_rows] + left_s[pl.ds(i, 1), :] + right_s[...]
        ).astype(BF16)
    for k in range(1, n):
        r_copy(k, seq).wait_send()


def local(
    n,
    tower,
    dna,
    dna_weight,
    conv_gain,
    depthwise_kernel,
    attn_gain,
    query_weight,
    key_weight,
    value_weight,
    out_weight,
    pair_in_weight,
    pair_weight,
):
    rows, channels = tower.shape
    block = query_weight.shape[0]
    depth = n * block
    chips = n // 2
    pair_width = pair_weight.shape[0]
    own_rows = rows // POOL
    all_rows = n * own_rows
    pieces = len(pieces_of(block)[0])
    dma = pltpu.SemaphoreType.DMA
    vmem = pl.BlockSpec(memory_space=pltpu.VMEM)
    anywhere = pl.BlockSpec(memory_space=pl.ANY)
    return pl.pallas_call(
        functools.partial(kernel, n),
        out_shape=(
            jax.ShapeDtypeStruct((rows, channels), BF16),
            jax.ShapeDtypeStruct((own_rows, all_rows, pair_width), BF16),
        ),
        in_specs=[vmem] * 6 + [anywhere] * 6,
        out_specs=(vmem, vmem),
        scratch_shapes=[
            pltpu.VMEM((depth, DK), BF16),
            pltpu.VMEM((n, DV, block), BF16),
            pltpu.VMEM((depth, H * DK), BF16),
            pltpu.VMEM((depth, out_weight.shape[1]), BF16),
            pltpu.VMEM(pair_in_weight.shape, BF16),
            pltpu.VMEM(pair_weight.shape, BF16),
            pltpu.VMEM((rows, channels), F32),
            pltpu.VMEM((rows + 2 * REACH, channels), F32),
            pltpu.VMEM((2, EDGE, channels), BF16),
            pltpu.VMEM((2, EDGE, channels), BF16),
            pltpu.VMEM((rows, channels), BF16),
            pltpu.VMEM((rows, channels), BF16),
            pltpu.VMEM((PAIRS, 2 * rows, DK), BF16),
            pltpu.VMEM((n * rows, DK), BF16),
            pltpu.VMEM((n * rows, DV), BF16),
            pltpu.VMEM((PAIRS, rows, 2 * DV), BF16),
            pltpu.VMEM((16, channels), F32),
            pltpu.VMEM((16, pair_width), F32),
            pltpu.VMEM((n, 16, pair_width), BF16),
            pltpu.VMEM((all_rows, pair_width), F32),
            pltpu.VMEM((own_rows * all_rows, pair_width), BF16),
            pltpu.VMEM((2, channels), F32),
            dma((4,)),
            dma((6,)),
            dma((2, 4)),
        ]
        + [dma((8, chips - 1, pieces))] * 2
        + [dma((2 * chips - 1, 2))] * 2
        + [dma((n - 1,))] * 2,
        compiler_params=pltpu.CompilerParams(
            collective_id=0, has_side_effects=True, vmem_limit_bytes=56 * 1024 * 1024
        ),
    )(
        tower,
        dna,
        dna_weight,
        conv_gain,
        depthwise_kernel,
        attn_gain,
        query_weight,
        key_weight,
        value_weight.T,
        out_weight,
        pair_in_weight,
        pair_weight,
    )


def solution(mesh):
    rows = P(("batch", "seq"), None)
    in_specs = (rows, rows, P(), P(), P(), P()) + (P("seq", None),) * 4 + (P(), P())
    out_specs = (rows, P(("batch", "seq"), None, None))
    return jax.shard_map(
        functools.partial(local, mesh.shape["seq"]),
        mesh=mesh,
        in_specs=in_specs,
        out_specs=out_specs,
        check_vma=False,
    )
```
